32 devices in a mesh: group: 1, expert: 32 (over z, y, x, core).
Axes of the slice: x: 2, y: 2, z: 4, core: 2. Of those that a mesh axis runs over, the one named last changes fastest.
Arguments:
- text_rows: bfloat16 [2048, 2560], P(('group', 'expert')), may hold values from -6 to 6
- image_rows: bfloat16 [64, 16, 2560], P(('group', 'expert')), may hold values from -6 to 6
- image_probe: bfloat16 [2560], replicated, may hold values from -0.125 to 0.125
- response_image: int32 [128], P(('group', 'expert')), may hold values from 0 to 63
- token_response: int32 [32, 64], P(('group', 'expert')), may hold values from 0 to 3, never falling along the last dimension, each value on 1 to 32 neighbouring positions
- norm_gain: bfloat16 [2560], replicated, may hold values from 0.5 to 1.5
- router_weight: bfloat16 [2560, 16], replicated, may hold values from -0.125 to 0.125
- expert_routes: int32 [2048, 6], P(('group', 'expert')), may hold values from 0 to 15, all different within a row; in each aligned block of 64 rows (0 to 63, 64 to 127, ...) at most 32 rows name the same one
- gate_weight: bfloat16 [32, 768, 2560], P('expert'), may hold values from -0.125 to 0.125
- up_weight: bfloat16 [32, 768, 2560], P('expert'), may hold values from -0.125 to 0.125
- down_weight: bfloat16 [32, 768, 2560], P('expert'), may hold values from -0.15625 to 0.15625
- reward_head: bfloat16 [2560], replicated, may hold values from -0.125 to 0.125
Outputs:
- token_output: bfloat16 [2048, 2560], P(('group', 'expert'))
- response_score: float32 [128], P(('group', 'expert'))
The draws below stay inside these ranges and needn't reach their ends.
Inputs may be any that keep to these rules, and one draw needn't show every extreme that they name: `expert_routes`: each row names 6 different experts. In the rows of one device, no expert is named by more than 32 rows, and in some device's rows some expert is named by exactly 32. `token_response`: along each device's row the value never falls; every response of the device has 1 to 32 tokens.
All inputs are finite; a program needn't handle non-finite values.
Results may differ from the reference program's by a relative error of at most 0.0046.
Values may be sent and summed in bfloat16 or wider, within the bound.
A program may use at most 64 MiB of HBM per device.

```python
import math
import jax
import jax.numpy as jnp
import numpy as np
from jax import lax

D = 2560
EXP_HID = 1536
HALF = 768
TOP = 6
TOK_DEV = 64
RESP_DEV = 4
V_ROWS = 16
EXPERTS = 16
CAP = 32
TOKENS = 2048
RESPONSES = 128
IMAGES = 64
N_EXPERT = 32


def touch_ends(drawn, key, least, top_value):
    index_at = [jax.random.randint(jax.random.fold_in(key, axis), (), 0, length) for axis, length in enumerate(drawn.shape)]
    widest = drawn.shape.index(max(drawn.shape))
    neighbour = index_at[:widest] + [(index_at[widest] + 1) % drawn.shape[widest]] + index_at[widest + 1:]
    return drawn.at[tuple(index_at)].set(least).at[tuple(neighbour)].set(top_value)


def block_levels(stream_key, dims, cuts, least, high):
    level, own = 1.0, jax.random.fold_in(stream_key, 6)
    for position, blocks in cuts:
        heights = jnp.exp(jax.random.uniform(jax.random.fold_in(own, position), (blocks,), jnp.float32, least / len(cuts), high / len(cuts)))
        level = level * jnp.repeat(heights, dims[position] // blocks).reshape([-1 if axis == position else 1 for axis in range(len(dims))])
    return level


def rank_table(amount, skew):
    portions = [(1 << 20) // math.isqrt(standing ** skew) + 1 for standing in range(1, amount + 1)]
    deviation = 1 + sum(portions) // (1 << 30)
    return np.cumsum(np.array([max(1, weight // deviation) for weight in portions]))


def ranked_ids(own_key, dims, count, slope):
    grid = rank_table(count, slope)
    ticket = jax.random.randint(jax.random.fold_in(own_key, 1), dims, 0, int(grid[count - 1]))
    grade = jnp.searchsorted(jnp.asarray(grid, jnp.int32), ticket, side="right")
    return jax.random.permutation(jax.random.fold_in(own_key, 2), count)[grade].astype(jnp.int32)


def split_up(count, total, limit, slope):
    weights = [(1 << 20) // math.isqrt(standing ** slope) + 1 for standing in range(2, count + 1)]
    rest, holding = total - limit - (count - 1), [1] * (count - 1)
    while rest > 0:
        free = [i for i in range(count - 1) if holding[i] < limit]
        pool, left = sum([weights[i] for i in free]), rest
        for i in free:
            extra = min(limit - holding[i], max(1, left * weights[i] // pool), rest)
            holding[i] = holding[i] + extra
            rest = rest - extra
    return np.array([limit] + holding)


def ragged_sizes(rng, number_of, total, reach, lean):
    if number_of == 2:
        one = jax.random.randint(rng, (), max(1, total - reach), min(reach, total - 1) + 1)
        return jnp.stack([one, total - one])
    tallies = jnp.asarray(split_up(number_of, total, reach, lean), jnp.int32)
    pairs = (number_of - 1) // 2
    source_of, taker = tallies[1:1 + 2 * pairs:2], tallies[2:2 + 2 * pairs:2]
    slack = jnp.minimum(source_of - 1, reach - taker)
    shifted = jax.random.randint(jax.random.fold_in(rng, 1), (pairs,), 0, 1 << 20) % (slack + 1)
    tallies = tallies.at[1:1 + 2 * pairs:2].set(source_of - shifted).at[2:2 + 2 * pairs:2].set(taker + shifted)
    return tallies[jax.random.permutation(jax.random.fold_in(rng, 2), number_of)]


def deal_out(own_key, own, number, rows, amount, top, limit, slope):
    order = jax.random.permutation(own_key, amount)
    packed, ordinary = load_shares(amount, rows * top, limit, slope, True), load_shares(amount, rows * top, limit, slope, False)
    places = jnp.arange(amount)

    def named(lengths, offset_by):
        used = int((lengths > 0).sum())
        fixed = max(1, used // 4)
        moved = fixed + (places - fixed + offset_by * (used - fixed)) % max(1, amount - fixed)
        return jnp.zeros((amount,), jnp.int32).at[order[jnp.where(places < fixed, places, moved)]].set(jnp.asarray(lengths, jnp.int32))

    lengths = jnp.where(number % 4 == 0, named(packed, number // 4), named(ordinary, number - number // 4 - 1))
    mixed = jax.random.permutation(jax.random.fold_in(own, 3), amount)
    donor, receiver = mixed[0:amount // 2 * 2:2], mixed[1:amount // 2 * 2:2]
    margin = jnp.minimum(lengths[donor] - 1, limit - lengths[receiver]) // 2
    margin = jnp.where((donor == order[0]) | (receiver == order[0]) | (lengths[receiver] == 0), 0, jnp.maximum(margin, 0))
    moved = jax.random.randint(jax.random.fold_in(own, 4), (amount // 2,), 0, 1 << 20) % (margin + 1)
    lengths = lengths.at[donor].add(-moved).at[receiver].add(moved)
    members = jnp.searchsorted(jnp.cumsum(lengths), jnp.arange(rows * top), side="right").astype(jnp.int32)
    listing = members.reshape(top, rows).T
    listing = listing[jax.random.permutation(jax.random.fold_in(own, 1), rows)]
    offset_by = jax.random.randint(jax.random.fold_in(own, 2), (rows, 1), 0, top)
    return jnp.take_along_axis(listing, (jnp.arange(top)[None, :] + offset_by) % top, axis=1)


def load_shares(count, total, bound, lean, full):
    loads = [(1 << 20) // math.isqrt(grade ** lean) + 1 for grade in range(1, count + 1)]
    largest = bound if full else min(bound, max(-(-total // count), total * loads[0] // sum(loads)))
    least = 1 if total - largest >= count - 1 else 0
    given, spare = [largest] + [least] * (count - 1), total - largest - least * (count - 1)
    while spare > 0:
        movable = [i for i in range(1, count) if given[i] < largest] or [i for i in range(1, count) if given[i] < bound]
        pool, budget = sum([loads[i] for i in movable]), spare
        for i in movable:
            more = min(bound - given[i], max(1, budget * loads[i] // pool), spare)
            given[i] = given[i] + more
            spare = spare - more
    return np.array(given)


def scatter_about(stream_key, dims, deviation, most, pieces=(), held_as=jnp.bfloat16):
    drawn = jax.random.normal(stream_key, dims, jnp.float32) * deviation
    if len(pieces) > 0:
        drawn = block_levels(stream_key, dims, pieces, -0.22, 0.18) * drawn
    return jnp.clip(drawn, min=-most, max=most).astype(held_as)


def setup_inputs(seed: int = 0, part: int = 0) -> dict:
    arg_keys = jax.random.split(jax.random.key(seed), 13)
    part_splits = jax.random.split(jax.random.fold_in(arg_keys[12], part), 13)
    text_rows = scatter_about(part_splits[0], (TOKENS, D), 1.0, 6.0, ((0, 32),))
    image_rows = scatter_about(part_splits[1], (IMAGES, V_ROWS, D), 1.0, 6.0, ((0, 32),))
    image_probe = scatter_about(arg_keys[2], (D,), D ** -0.5, 0.125)
    response_image = touch_ends(ranked_ids(part_splits[3], (RESPONSES,), IMAGES, 2), jax.random.fold_in(part_splits[3], 3), 0, IMAGES - 1).astype(jnp.int32)
    token_response = jax.vmap(lambda own: jnp.searchsorted(jnp.cumsum(ragged_sizes(own, RESP_DEV, TOK_DEV, TOK_DEV // 2, 1)), jnp.arange(TOK_DEV), side="right"))(jax.random.split(part_splits[4], N_EXPERT)).reshape((N_EXPERT, TOK_DEV)).astype(jnp.int32)
    norm_gain = jnp.clip(1.0 + 0.1 * jax.random.normal(arg_keys[5], (D,), jnp.float32), 0.5, 1.5).astype(jnp.bfloat16)
    router_weight = scatter_about(arg_keys[6], (D, EXPERTS), D ** -0.5, 0.125)
    expert_routes_keys = jax.random.split(jax.random.fold_in(part_splits[7], 1), TOKENS // TOK_DEV)
    expert_routes_turns = jax.random.permutation(jax.random.fold_in(part_splits[7], 3), TOKENS // TOK_DEV)
    expert_routes = jax.vmap(lambda own, number: deal_out(jax.random.fold_in(part_splits[7], 2), own, number, TOK_DEV, EXPERTS, TOP, CAP, 2))(expert_routes_keys, expert_routes_turns).reshape((TOKENS, TOP))
    gate_weight = scatter_about(arg_keys[8], (N_EXPERT, HALF, D), D ** -0.5, 0.125, ((0, 32),))
    up_weight = scatter_about(arg_keys[9], (N_EXPERT, HALF, D), D ** -0.5, 0.125, ((0, 32),))
    down_weight = scatter_about(arg_keys[10], (N_EXPERT, HALF, D), EXP_HID ** -0.5, 0.15625, ((0, 32),))
    reward_head = scatter_about(arg_keys[11], (D,), D ** -0.5, 0.125)
    return {"text_rows": text_rows, "image_rows": image_rows, "image_probe": image_probe, "response_image": response_image, "token_response": token_response, "norm_gain": norm_gain, "router_weight": router_weight, "expert_routes": expert_routes, "gate_weight": gate_weight, "up_weight": up_weight, "down_weight": down_weight, "reward_head": reward_head}


epsilon = 1e-06

def slot_tables(route_block, weight_block, first_token):
    routed = route_block.reshape(-1)
    member = (routed[:, None] == jnp.arange(EXPERTS, dtype=jnp.int32)[None, :]).astype(jnp.int32)
    earlier = jnp.cumsum(member, axis=0) - member
    places = routed * CAP + lax.optimization_barrier(jnp.sum(earlier * member, axis=1))
    owners = first_token + jnp.arange(routed.shape[0], dtype=jnp.int32) // TOP + 1
    slot_token = jnp.zeros((EXPERTS * CAP,), jnp.int32).at[places].set(owners)
    slot_weight = jnp.zeros((EXPERTS * CAP,), weight_block.dtype).at[places].set(weight_block.reshape(-1))
    return (slot_token, slot_weight)

def expert_half(inputs, gate_rows, up_rows, down_rows):
    gate_value = jnp.dot(inputs, gate_rows.T, preferred_element_type=jnp.float32)
    up_value = jnp.dot(inputs, up_rows.T, preferred_element_type=jnp.float32)
    active = (jax.nn.silu(gate_value) * up_value).astype(jnp.bfloat16)
    return jnp.dot(active, down_rows, preferred_element_type=jnp.float32).astype(jnp.bfloat16)

def reference(text_rows, image_rows, image_probe, response_image, token_response, norm_gain, router_weight, expert_routes, gate_weight, up_weight, down_weight, reward_head):
    probe_score = jnp.einsum('ivd,d->iv', image_rows.astype(jnp.float32), image_probe.astype(jnp.float32))
    pool_weight = jax.nn.sigmoid(probe_score).astype(jnp.bfloat16)
    pooled = (jnp.einsum('iv,ivd->id', pool_weight.astype(jnp.float32), image_rows.astype(jnp.float32)) / math.sqrt(V_ROWS)).astype(jnp.bfloat16)
    global_response = (jnp.arange(N_EXPERT, dtype=jnp.int32)[:, None] * RESP_DEV + token_response).reshape(-1)
    context = pooled[response_image[global_response]].astype(jnp.float32)
    hidden_state = text_rows.astype(jnp.float32) + context
    inverse = lax.rsqrt(lax.optimization_barrier(jnp.mean(hidden_state * hidden_state, axis=-1, keepdims=True)) + epsilon)
    normed = (hidden_state * inverse * norm_gain.astype(jnp.float32)).astype(jnp.bfloat16)
    logits = jnp.dot(normed, router_weight, preferred_element_type=jnp.float32)
    chosen = jax.nn.sigmoid(jnp.take_along_axis(logits, expert_routes, axis=1))
    route_weight = chosen / lax.optimization_barrier(jnp.sum(chosen, axis=1, keepdims=True))
    starts = jnp.arange(N_EXPERT, dtype=jnp.int32) * TOK_DEV
    slot_token, slot_weight = jax.vmap(slot_tables)(expert_routes.reshape(N_EXPERT, TOK_DEV, TOP), route_weight.reshape(N_EXPERT, TOK_DEV, TOP), starts)
    padded = jnp.concatenate([jnp.zeros((1, D), jnp.bfloat16), normed], axis=0)

    def expert_step(mixture, expert):
        picked = lax.dynamic_slice_in_dim(slot_token, expert * CAP, CAP, 1).reshape(-1)
        scaled = lax.dynamic_slice_in_dim(slot_weight, expert * CAP, CAP, 1).reshape(-1)
        inputs = padded[picked]
        first_half = expert_half(inputs, gate_weight[2 * expert], up_weight[2 * expert], down_weight[2 * expert])
        second_half = expert_half(inputs, gate_weight[2 * expert + 1], up_weight[2 * expert + 1], down_weight[2 * expert + 1])
        output = (first_half.astype(jnp.float32) + second_half.astype(jnp.float32)).astype(jnp.bfloat16)
        return (mixture.at[picked].add(scaled[:, None] * output.astype(jnp.float32)), None)
    mixture = lax.scan(expert_step, jnp.zeros((TOKENS + 1, D), jnp.float32), jnp.arange(EXPERTS, dtype=jnp.int32))[0]
    combined = hidden_state + mixture[1:]
    token_output = combined.astype(jnp.bfloat16)
    reward = lax.optimization_barrier(jnp.sum(combined * reward_head.astype(jnp.float32), axis=-1))
    totals = jax.ops.segment_sum(reward, global_response, num_segments=RESPONSES)
    counts = jax.ops.segment_sum(jnp.ones_like(reward), global_response, num_segments=RESPONSES)
    return (token_output, totals / counts)
```

```python
import math

import jax
import jax.numpy as jnp
from jax import lax
from jax.sharding import PartitionSpec as P

epsilon = 1e-06


def expert_half(inputs, gate_rows, up_rows, down_rows):
    contract = (((1,), (1,)), ((), ()))
    gate_value = lax.dot_general(inputs, gate_rows, contract, preferred_element_type=jnp.float32)
    up_value = lax.dot_general(inputs, up_rows, contract, preferred_element_type=jnp.float32)
    active = (jax.nn.silu(gate_value) * up_value).astype(jnp.bfloat16)
    return jnp.dot(active, down_rows, preferred_element_type=jnp.float32)


def exchange(blocks):
    return lax.all_to_all(blocks, "expert", split_axis=0, concat_axis=0, tiled=True)


def body(
    text_rows,
    image_rows,
    image_probe,
    response_image,
    token_response,
    norm_gain,
    router_weight,
    expert_routes,
    gate_weight,
    up_weight,
    down_weight,
    reward_head,
):
    token_count, feature_count = text_rows.shape
    top_count = expert_routes.shape[1]
    expert_count = router_weight.shape[1]
    capacity = min(token_count, 4 * token_count * top_count // (3 * expert_count))
    device_count = lax.axis_size("expert")
    response_count = response_image.shape[0]
    probe_score = jnp.einsum(
        "ivd,d->iv", image_rows, image_probe, preferred_element_type=jnp.float32
    )
    pool_weight = jax.nn.sigmoid(probe_score).astype(jnp.bfloat16)
    pooled_sum = jnp.einsum(
        "iv,ivd->id", pool_weight, image_rows, preferred_element_type=jnp.float32
    )
    pooled = (pooled_sum / math.sqrt(image_rows.shape[1])).astype(jnp.bfloat16)
    copies = jnp.broadcast_to(pooled[None], (device_count,) + pooled.shape)
    shard_rows = exchange(copies).reshape(-1, feature_count)
    image_ids = jnp.arange(shard_rows.shape[0], dtype=jnp.int32)
    choose = (response_image[:, None] == image_ids[None, :]).astype(jnp.bfloat16)
    response_context = jnp.dot(choose, shard_rows, preferred_element_type=jnp.float32).astype(
        jnp.bfloat16
    )
    response_onehot = (
        token_response[0][:, None] == jnp.arange(response_count, dtype=jnp.int32)[None, :]
    )
    token_context = jnp.dot(
        response_onehot.astype(jnp.bfloat16), response_context, preferred_element_type=jnp.float32
    )
    hidden_state = text_rows.astype(jnp.float32) + token_context
    inverse = lax.rsqrt(jnp.mean(hidden_state * hidden_state, axis=-1, keepdims=True) + epsilon)
    normed = (hidden_state * inverse * norm_gain.astype(jnp.float32)).astype(jnp.bfloat16)
    logits = jnp.dot(normed, router_weight, preferred_element_type=jnp.float32)
    expert_ids = jnp.arange(expert_count, dtype=jnp.int32)
    member = jnp.any(expert_routes[:, :, None] == expert_ids[None, None, :], axis=1)
    chosen = jnp.where(member, jax.nn.sigmoid(logits), 0.0)
    route_weight = chosen / jnp.sum(chosen, axis=1, keepdims=True)
    positions = jnp.arange(token_count, dtype=jnp.int32)
    before = (positions[None, :] < positions[:, None]).astype(jnp.bfloat16)
    place = jnp.dot(before, member.astype(jnp.bfloat16), preferred_element_type=jnp.float32)
    slot_ids = jnp.arange(capacity, dtype=jnp.int32).astype(jnp.float32)
    taken = member[:, :, None] & (place[:, :, None] == slot_ids[None, None, :])
    slot_total = expert_count * capacity
    spread = taken.astype(jnp.bfloat16).reshape(token_count, slot_total)
    blend = jnp.where(taken, route_weight[:, :, None], 0.0).reshape(token_count, slot_total)
    outgoing = lax.dot_general(
        spread, normed, (((0,), (0,)), ((), ())), preferred_element_type=jnp.float32
    ).astype(jnp.bfloat16)
    share = slot_total // device_count
    swap = [(device, device ^ 1) for device in range(device_count)]
    weights = (gate_weight[0], up_weight[0], down_weight[0])
    mine = exchange(outgoing.reshape(device_count, share, feature_count))
    mine = mine.reshape(device_count * share, feature_count)
    other = lax.ppermute(mine, "expert", swap)
    own_part = expert_half(mine, *weights).astype(jnp.bfloat16)
    other_part = expert_half(other, *weights).astype(jnp.bfloat16)
    arrived_part = lax.ppermute(other_part, "expert", swap)
    summed = (own_part.astype(jnp.float32) + arrived_part.astype(jnp.float32)).astype(jnp.bfloat16)
    outputs = exchange(summed.reshape(device_count, share, feature_count))
    outputs = outputs.reshape(slot_total, feature_count)
    blend_high = blend.astype(jnp.bfloat16)
    blend_low = (blend - blend_high.astype(jnp.float32)).astype(jnp.bfloat16)
    mixture = jnp.dot(blend_high, outputs, preferred_element_type=jnp.float32)
    mixture = mixture + jnp.dot(blend_low, outputs, preferred_element_type=jnp.float32)
    combined = hidden_state + mixture
    reward = jnp.sum(combined * reward_head.astype(jnp.float32), axis=-1)
    totals = jnp.sum(jnp.where(response_onehot, reward[:, None], 0.0), axis=0)
    counts = jnp.sum(response_onehot.astype(jnp.float32), axis=0)
    return (combined.astype(jnp.bfloat16), totals / counts)


def solution(mesh):
    in_specs = (
        P(("group", "expert"), None),
        P(("group", "expert"), None, None),
        P(),
        P(("group", "expert")),
        P(("group", "expert"), None),
        P(),
        P(),
        P(("group", "expert"), None),
        P("expert", None, None),
        P("expert", None, None),
        P("expert", None, None),
        P(),
    )
    out_specs = (P(("group", "expert"), None), P(("group", "expert")))
    return jax.shard_map(body, mesh=mesh, in_specs=in_specs, out_specs=out_specs, check_vma=False)
```

```python
import math

import jax
import jax.numpy as jnp
from jax import lax
from jax.sharding import PartitionSpec as P

epsilon = 1e-06


def expert_half(inputs, gate_rows, up_rows, down_rows):
    contract = (((1,), (1,)), ((), ()))
    gate_value = lax.dot_general(inputs, gate_rows, contract, preferred_element_type=jnp.float32)
    up_value = lax.dot_general(inputs, up_rows, contract, preferred_element_type=jnp.float32)
    active = (jax.nn.silu(gate_value) * up_value).astype(jnp.bfloat16)
    active = lax.optimization_barrier(active)
    return jnp.dot(active, down_rows, preferred_element_type=jnp.float32)


def exchange(blocks, groups=None):
    return lax.all_to_all(
        blocks, "expert", split_axis=0, concat_axis=0, axis_index_groups=groups, tiled=True
    )


def slot_onehot(routes, first_expert, side_experts, capacity):
    token_count = routes.shape[0]
    expert_ids = first_expert + jnp.arange(side_experts, dtype=jnp.int32)
    member = jnp.any(routes[:, :, None] == expert_ids[None, None, :], axis=1)
    positions = jnp.arange(token_count, dtype=jnp.int32)
    before = (positions[None, :] < positions[:, None]).astype(jnp.bfloat16)
    place = jnp.dot(before, member.astype(jnp.bfloat16), preferred_element_type=jnp.float32)
    slot_ids = jnp.arange(capacity, dtype=jnp.int32).astype(jnp.float32)
    return member[:, :, None] & (place[:, :, None] == slot_ids[None, None, :])


def slot_blend(taken, normed, routes, router_weight, first_expert):
    token_count, side_experts, capacity = taken.shape
    logits = jnp.dot(normed, router_weight, preferred_element_type=jnp.float32)
    expert_ids = jnp.arange(router_weight.shape[1], dtype=jnp.int32)
    member = jnp.any(routes[:, :, None] == expert_ids[None, None, :], axis=1)
    chosen = jnp.where(member, jax.nn.sigmoid(logits), 0.0)
    route_weight = chosen / jnp.sum(chosen, axis=1, keepdims=True)
    route_weight = lax.dynamic_slice_in_dim(route_weight, first_expert, side_experts, axis=1)
    high = route_weight.astype(jnp.bfloat16)
    low = (route_weight - high.astype(jnp.float32)).astype(jnp.bfloat16)
    zero = jnp.zeros((), jnp.bfloat16)
    flat = (token_count, side_experts * capacity)
    return tuple(jnp.where(taken, part[:, :, None], zero).reshape(flat) for part in (high, low))


def fill_slots(taken, normed):
    spread = taken.astype(jnp.bfloat16).reshape(taken.shape[0], -1)
    return lax.dot_general(
        spread, normed, (((0,), (0,)), ((), ())), preferred_element_type=jnp.float32
    ).astype(jnp.bfloat16)


def run_expert(mine, swap, weights):
    rows = mine.shape[0]
    other = lax.ppermute(mine, "expert", swap)
    parts = expert_half(jnp.concatenate([mine, other], axis=0), *weights).astype(jnp.bfloat16)
    arrived = lax.ppermute(parts[rows:], "expert", swap)
    return (parts[:rows].astype(jnp.float32) + arrived.astype(jnp.float32)).astype(jnp.bfloat16)


def mix(blend, outputs):
    high, low = blend
    return jnp.dot(high, outputs, preferred_element_type=jnp.float32) + jnp.dot(
        low, outputs, preferred_element_type=jnp.float32
    )


def body(
    text_rows,
    image_rows,
    image_probe,
    response_image,
    token_response,
    norm_gain,
    router_weight,
    expert_routes,
    gate_weight,
    up_weight,
    down_weight,
    reward_head,
):
    token_count, feature_count = text_rows.shape
    top_count = expert_routes.shape[1]
    expert_count = router_weight.shape[1]
    capacity = min(token_count, 4 * token_count * top_count // (3 * expert_count))
    device_count = lax.axis_size("expert")
    response_count = response_image.shape[0]
    probe_score = jnp.einsum(
        "ivd,d->iv", image_rows, image_probe, preferred_element_type=jnp.float32
    )
    pool_weight = jax.nn.sigmoid(probe_score).astype(jnp.bfloat16)
    pooled_sum = jnp.einsum(
        "iv,ivd->id", pool_weight, image_rows, preferred_element_type=jnp.float32
    )
    pooled = (pooled_sum / math.sqrt(image_rows.shape[1])).astype(jnp.bfloat16)
    copies = jnp.broadcast_to(pooled[None], (device_count,) + pooled.shape)
    shard_rows = exchange(copies).reshape(-1, feature_count)
    image_ids = jnp.arange(shard_rows.shape[0], dtype=jnp.int32)
    choose = (response_image[:, None] == image_ids[None, :]).astype(jnp.bfloat16)
    response_context = jnp.dot(choose, shard_rows, preferred_element_type=jnp.float32).astype(
        jnp.bfloat16
    )
    response_onehot = (
        token_response[0][:, None] == jnp.arange(response_count, dtype=jnp.int32)[None, :]
    )
    token_context = jnp.dot(
        response_onehot.astype(jnp.bfloat16), response_context, preferred_element_type=jnp.float32
    )
    hidden_state = text_rows.astype(jnp.float32) + token_context
    inverse = lax.rsqrt(jnp.mean(hidden_state * hidden_state, axis=-1, keepdims=True) + epsilon)
    normed = (hidden_state * inverse * norm_gain.astype(jnp.float32)).astype(jnp.bfloat16)
    side_experts = expert_count // 2
    half = device_count // 2
    first_expert = (lax.axis_index("expert") // half) * side_experts
    across = [(device, (device + half) % device_count) for device in range(device_count)]
    sides = [list(range(half)), list(range(half, device_count))]
    swap = [(device, device ^ 1) for device in range(device_count)]
    weights = (gate_weight[0], up_weight[0], down_weight[0])
    far_routes = lax.ppermute(expert_routes, "expert", across)
    far_normed = lax.ppermute(normed, "expert", across)
    near_taken = slot_onehot(expert_routes, first_expert, side_experts, capacity)
    far_taken = slot_onehot(far_routes, first_expert, side_experts, capacity)
    slot_total = side_experts * capacity
    blocks = (half, slot_total // half, feature_count)
    flat = (slot_total, feature_count)
    near_in = exchange(fill_slots(near_taken, normed).reshape(blocks), sides).reshape(flat)
    far_in = exchange(fill_slots(far_taken, far_normed).reshape(blocks), sides).reshape(flat)
    near_sum = run_expert(near_in, swap, weights)
    far_sum = run_expert(far_in, swap, weights)
    near_sum, far_sum = lax.optimization_barrier((near_sum, far_sum))
    far_out = exchange(far_sum.reshape(blocks), sides).reshape(flat)
    near_out = exchange(near_sum.reshape(blocks), sides).reshape(flat)
    far_blend = slot_blend(far_taken, far_normed, far_routes, router_weight, first_expert)
    near_blend = slot_blend(near_taken, normed, expert_routes, router_weight, first_expert)
    far_mixture = lax.ppermute(mix(far_blend, far_out).astype(jnp.bfloat16), "expert", across)
    mixture = mix(near_blend, near_out) + far_mixture.astype(jnp.float32)
    combined = hidden_state + mixture
    reward = jnp.sum(combined * reward_head.astype(jnp.float32), axis=-1)
    totals = jnp.sum(jnp.where(response_onehot, reward[:, None], 0.0), axis=0)
    counts = jnp.sum(response_onehot.astype(jnp.float32), axis=0)
    return (combined.astype(jnp.bfloat16), totals / counts)


def solution(mesh):
    in_specs = (
        P(("group", "expert"), None),
        P(("group", "expert"), None, None),
        P(),
        P(("group", "expert")),
        P(("group", "expert"), None),
        P(),
        P(),
        P(("group", "expert"), None),
        P("expert", None, None),
        P("expert", None, None),
        P("expert", None, None),
        P(),
    )
    out_specs = (P(("group", "expert"), None), P(("group", "expert")))
    return jax.shard_map(body, mesh=mesh, in_specs=in_specs, out_specs=out_specs, check_vma=False)
```

```python
import math

import jax
import jax.numpy as jnp
from jax import lax
from jax.sharding import PartitionSpec as P

epsilon = 1e-06


def expert_half(inputs, gate_rows, up_rows, down_rows):
    contract = (((1,), (1,)), ((), ()))
    gate_value = lax.dot_general(inputs, gate_rows, contract, preferred_element_type=jnp.float32)
    up_value = lax.dot_general(inputs, up_rows, contract, preferred_element_type=jnp.float32)
    active = (jax.nn.silu(gate_value) * up_value).astype(jnp.bfloat16)
    active = lax.optimization_barrier(active)
    return jnp.dot(active, down_rows, preferred_element_type=jnp.float32)


def exchange(blocks, groups=None):
    return lax.all_to_all(
        blocks, "expert", split_axis=0, concat_axis=0, axis_index_groups=groups, tiled=True
    )


def slot_onehot(routes, first_expert, side_experts, capacity):
    token_count = routes.shape[0]
    expert_ids = first_expert + jnp.arange(side_experts, dtype=jnp.int32)
    member = jnp.any(routes[:, :, None] == expert_ids[None, None, :], axis=1)
    positions = jnp.arange(token_count, dtype=jnp.int32)
    before = (positions[None, :] < positions[:, None]).astype(jnp.bfloat16)
    place = jnp.dot(before, member.astype(jnp.bfloat16), preferred_element_type=jnp.float32)
    slot_ids = jnp.arange(capacity, dtype=jnp.int32).astype(jnp.float32)
    return member[:, :, None] & (place[:, :, None] == slot_ids[None, None, :])


def slot_blend(taken, normed, routes, router_weight, first_expert):
    token_count, side_experts, capacity = taken.shape
    logits = jnp.dot(normed, router_weight, preferred_element_type=jnp.float32)
    expert_ids = jnp.arange(router_weight.shape[1], dtype=jnp.int32)
    member = jnp.any(routes[:, :, None] == expert_ids[None, None, :], axis=1)
    chosen = jnp.where(member, jax.nn.sigmoid(logits), 0.0)
    route_weight = chosen / jnp.sum(chosen, axis=1, keepdims=True)
    route_weight = lax.dynamic_slice_in_dim(route_weight, first_expert, side_experts, axis=1)
    high = route_weight.astype(jnp.bfloat16)
    low = (route_weight - high.astype(jnp.float32)).astype(jnp.bfloat16)
    zero = jnp.zeros((), jnp.bfloat16)
    flat = (token_count, side_experts * capacity)
    return tuple(jnp.where(taken, part[:, :, None], zero).reshape(flat) for part in (high, low))


def fill_slots(taken, normed):
    spread = taken.astype(jnp.bfloat16).reshape(taken.shape[0], -1)
    return lax.dot_general(
        spread, normed, (((0,), (0,)), ((), ())), preferred_element_type=jnp.float32
    ).astype(jnp.bfloat16)


def both_cores(mine, swap):
    return jnp.concatenate([mine, lax.ppermute(mine, "expert", swap)], axis=0)


def run_expert(inputs, swap, weights):
    rows = inputs.shape[0] // 2
    parts = expert_half(inputs, *weights).astype(jnp.bfloat16)
    arrived = lax.ppermute(parts[rows:], "expert", swap)
    return (parts[:rows].astype(jnp.float32) + arrived.astype(jnp.float32)).astype(jnp.bfloat16)


def mix(blend, outputs):
    high, low = blend
    return jnp.dot(high, outputs, preferred_element_type=jnp.float32) + jnp.dot(
        low, outputs, preferred_element_type=jnp.float32
    )


def body(
    text_rows,
    image_rows,
    image_probe,
    response_image,
    token_response,
    norm_gain,
    router_weight,
    expert_routes,
    gate_weight,
    up_weight,
    down_weight,
    reward_head,
):
    token_count, feature_count = text_rows.shape
    top_count = expert_routes.shape[1]
    expert_count = router_weight.shape[1]
    capacity = min(token_count, 4 * token_count * top_count // (3 * expert_count))
    device_count = lax.axis_size("expert")
    response_count = response_image.shape[0]
    probe_score = jnp.einsum(
        "ivd,d->iv", image_rows, image_probe, preferred_element_type=jnp.float32
    )
    pool_weight = jax.nn.sigmoid(probe_score).astype(jnp.bfloat16)
    pooled_sum = jnp.einsum(
        "iv,ivd->id", pool_weight, image_rows, preferred_element_type=jnp.float32
    )
    pooled = (pooled_sum / math.sqrt(image_rows.shape[1])).astype(jnp.bfloat16)
    copies = jnp.broadcast_to(pooled[None], (device_count,) + pooled.shape)
    shard_rows = exchange(copies).reshape(-1, feature_count)
    image_ids = jnp.arange(shard_rows.shape[0], dtype=jnp.int32)
    choose = (response_image[:, None] == image_ids[None, :]).astype(jnp.bfloat16)
    response_context = jnp.dot(choose, shard_rows, preferred_element_type=jnp.float32).astype(
        jnp.bfloat16
    )
    response_onehot = (
        token_response[0][:, None] == jnp.arange(response_count, dtype=jnp.int32)[None, :]
    )
    token_context = jnp.dot(
        response_onehot.astype(jnp.bfloat16), response_context, preferred_element_type=jnp.float32
    )
    hidden_state = text_rows.astype(jnp.float32) + token_context
    inverse = lax.rsqrt(jnp.mean(hidden_state * hidden_state, axis=-1, keepdims=True) + epsilon)
    normed = (hidden_state * inverse * norm_gain.astype(jnp.float32)).astype(jnp.bfloat16)
    side_experts = expert_count // 2
    half = device_count // 2
    first_expert = (lax.axis_index("expert") // half) * side_experts
    across = [(device, (device + half) % device_count) for device in range(device_count)]
    sides = [list(range(half)), list(range(half, device_count))]
    swap = [(device, device ^ 1) for device in range(device_count)]
    weights = (gate_weight[0], up_weight[0], down_weight[0])
    far_routes = lax.ppermute(expert_routes, "expert", across)
    far_normed = lax.ppermute(normed, "expert", across)
    near_taken = slot_onehot(expert_routes, first_expert, side_experts, capacity)
    far_taken = slot_onehot(far_routes, first_expert, side_experts, capacity)
    slot_total = side_experts * capacity
    blocks = (half, slot_total // half, feature_count)
    flat = (slot_total, feature_count)
    near_in = exchange(fill_slots(near_taken, normed).reshape(blocks), sides).reshape(flat)
    far_slots = fill_slots(far_taken, far_normed).reshape(blocks)
    near_in, far_slots = lax.optimization_barrier((both_cores(near_in, swap), far_slots))
    far_in = exchange(far_slots, sides).reshape(flat)
    near_sum = run_expert(near_in, swap, weights)
    far_sum = run_expert(both_cores(far_in, swap), swap, weights)
    near_sum, far_sum = lax.optimization_barrier((near_sum, far_sum))
    far_out = exchange(far_sum.reshape(blocks), sides).reshape(flat)
    near_out = exchange(near_sum.reshape(blocks), sides).reshape(flat)
    far_blend = slot_blend(far_taken, far_normed, far_routes, router_weight, first_expert)
    near_blend = slot_blend(near_taken, normed, expert_routes, router_weight, first_expert)
    far_mixture = lax.ppermute(mix(far_blend, far_out).astype(jnp.bfloat16), "expert", across)
    mixture = mix(near_blend, near_out) + far_mixture.astype(jnp.float32)
    combined = hidden_state + mixture
    reward = jnp.sum(combined * reward_head.astype(jnp.float32), axis=-1)
    totals = jnp.sum(jnp.where(response_onehot, reward[:, None], 0.0), axis=0)
    counts = jnp.sum(response_onehot.astype(jnp.float32), axis=0)
    return (combined.astype(jnp.bfloat16), totals / counts)


def solution(mesh):
    in_specs = (
        P(("group", "expert"), None),
        P(("group", "expert"), None, None),
        P(),
        P(("group", "expert")),
        P(("group", "expert"), None),
        P(),
        P(),
        P(("group", "expert"), None),
        P("expert", None, None),
        P("expert", None, None),
        P("expert", None, None),
        P(),
    )
    out_specs = (P(("group", "expert"), None), P(("group", "expert")))
    return jax.shard_map(body, mesh=mesh, in_specs=in_specs, out_specs=out_specs, check_vma=False)
```

```python
import math

import jax
import jax.numpy as jnp
from jax import lax
from jax.sharding import PartitionSpec as P

epsilon = 1e-06


def expert_half(inputs, gate_rows, up_rows, down_rows):
    contract = (((1,), (1,)), ((), ()))
    gate_value = lax.dot_general(inputs, gate_rows, contract, preferred_element_type=jnp.float32)
    up_value = lax.dot_general(inputs, up_rows, contract, preferred_element_type=jnp.float32)
    active = (jax.nn.silu(gate_value) * up_value).astype(jnp.bfloat16)
    active = lax.optimization_barrier(active)
    return jnp.dot(active, down_rows, preferred_element_type=jnp.float32).astype(jnp.bfloat16)


def exchange(blocks, groups=None):
    return lax.all_to_all(
        blocks, "expert", split_axis=0, concat_axis=0, axis_index_groups=groups, tiled=True
    )


def slot_onehot(routes, first_expert, side_experts, capacity):
    token_count = routes.shape[0]
    expert_ids = first_expert + jnp.arange(side_experts, dtype=jnp.int32)
    member = jnp.any(routes[:, :, None] == expert_ids[None, None, :], axis=1)
    positions = jnp.arange(token_count, dtype=jnp.int32)
    before = (positions[None, :] < positions[:, None]).astype(jnp.bfloat16)
    place = jnp.dot(before, member.astype(jnp.bfloat16), preferred_element_type=jnp.float32)
    slot_ids = jnp.arange(capacity, dtype=jnp.int32).astype(jnp.float32)
    return member[:, :, None] & (place[:, :, None] == slot_ids[None, None, :])


def slot_blend(taken, normed, routes, router_weight, first_expert):
    token_count, side_experts, capacity = taken.shape
    logits = jnp.dot(normed, router_weight, preferred_element_type=jnp.float32)
    expert_ids = jnp.arange(router_weight.shape[1], dtype=jnp.int32)
    member = jnp.any(routes[:, :, None] == expert_ids[None, None, :], axis=1)
    chosen = jnp.where(member, jax.nn.sigmoid(logits), 0.0)
    route_weight = chosen / jnp.sum(chosen, axis=1, keepdims=True)
    route_weight = lax.dynamic_slice_in_dim(route_weight, first_expert, side_experts, axis=1)
    high = route_weight.astype(jnp.bfloat16)
    low = (route_weight - high.astype(jnp.float32)).astype(jnp.bfloat16)
    zero = jnp.zeros((), jnp.bfloat16)
    flat = (token_count, side_experts * capacity)
    return tuple(jnp.where(taken, part[:, :, None], zero).reshape(flat) for part in (high, low))


def fill_slots(taken, normed):
    spread = taken.astype(jnp.bfloat16).reshape(taken.shape[0], -1)
    return lax.dot_general(
        spread, normed, (((0,), (0,)), ((), ())), preferred_element_type=jnp.float32
    ).astype(jnp.bfloat16)


def both_cores(mine, swap):
    return jnp.concatenate([mine, lax.ppermute(mine, "expert", swap)], axis=0)


def sum_cores(parts, swap):
    rows = parts.shape[0] // 2
    arrived = lax.ppermute(parts[rows:], "expert", swap)
    return (parts[:rows].astype(jnp.float32) + arrived.astype(jnp.float32)).astype(jnp.bfloat16)


def mix(blend, outputs):
    high, low = blend
    return jnp.dot(high, outputs, preferred_element_type=jnp.float32) + jnp.dot(
        low, outputs, preferred_element_type=jnp.float32
    )


def body(
    text_rows,
    image_rows,
    image_probe,
    response_image,
    token_response,
    norm_gain,
    router_weight,
    expert_routes,
    gate_weight,
    up_weight,
    down_weight,
    reward_head,
):
    token_count, feature_count = text_rows.shape
    top_count = expert_routes.shape[1]
    expert_count = router_weight.shape[1]
    capacity = min(token_count, 4 * token_count * top_count // (3 * expert_count))
    device_count = lax.axis_size("expert")
    response_count = response_image.shape[0]
    probe_score = jnp.einsum(
        "ivd,d->iv", image_rows, image_probe, preferred_element_type=jnp.float32
    )
    pool_weight = jax.nn.sigmoid(probe_score).astype(jnp.bfloat16)
    pooled_sum = jnp.einsum(
        "iv,ivd->id", pool_weight, image_rows, preferred_element_type=jnp.float32
    )
    pooled = (pooled_sum / math.sqrt(image_rows.shape[1])).astype(jnp.bfloat16)
    copies = jnp.broadcast_to(pooled[None], (device_count,) + pooled.shape)
    shard_rows = exchange(copies).reshape(-1, feature_count)
    image_ids = jnp.arange(shard_rows.shape[0], dtype=jnp.int32)
    choose = (response_image[:, None] == image_ids[None, :]).astype(jnp.bfloat16)
    response_context = jnp.dot(choose, shard_rows, preferred_element_type=jnp.float32).astype(
        jnp.bfloat16
    )
    response_onehot = (
        token_response[0][:, None] == jnp.arange(response_count, dtype=jnp.int32)[None, :]
    )
    token_context = jnp.dot(
        response_onehot.astype(jnp.bfloat16), response_context, preferred_element_type=jnp.float32
    )
    hidden_state = text_rows.astype(jnp.float32) + token_context
    inverse = lax.rsqrt(jnp.mean(hidden_state * hidden_state, axis=-1, keepdims=True) + epsilon)
    normed = (hidden_state * inverse * norm_gain.astype(jnp.float32)).astype(jnp.bfloat16)
    side_experts = expert_count // 2
    half = device_count // 2
    first_expert = (lax.axis_index("expert") // half) * side_experts
    across = [(device, (device + half) % device_count) for device in range(device_count)]
    sides = [list(range(half)), list(range(half, device_count))]
    swap = [(device, device ^ 1) for device in range(device_count)]
    weights = (gate_weight[0], up_weight[0], down_weight[0])
    far_routes = lax.ppermute(expert_routes, "expert", across)
    far_normed = lax.ppermute(normed, "expert", across)
    near_taken = slot_onehot(expert_routes, first_expert, side_experts, capacity)
    far_taken = slot_onehot(far_routes, first_expert, side_experts, capacity)
    slot_total = side_experts * capacity
    blocks = (half, slot_total // half, feature_count)
    flat = (slot_total, feature_count)
    near_in = exchange(fill_slots(near_taken, normed).reshape(blocks), sides).reshape(flat)
    far_slots = fill_slots(far_taken, far_normed).reshape(blocks)
    near_in, far_slots = lax.optimization_barrier((near_in, far_slots))
    near_in, far_slots = lax.optimization_barrier((both_cores(near_in, swap), far_slots))
    far_in = exchange(far_slots, sides).reshape(flat)
    near_parts = expert_half(near_in, *weights)
    near_parts, far_in = lax.optimization_barrier((near_parts, far_in))
    near_sum = sum_cores(near_parts, swap)
    far_sum = sum_cores(expert_half(both_cores(far_in, swap), *weights), swap)
    near_sum, far_sum = lax.optimization_barrier((near_sum, far_sum))
    far_out = exchange(far_sum.reshape(blocks), sides).reshape(flat)
    near_out = exchange(near_sum.reshape(blocks), sides).reshape(flat)
    far_blend = slot_blend(far_taken, far_normed, far_routes, router_weight, first_expert)
    near_blend = slot_blend(near_taken, normed, expert_routes, router_weight, first_expert)
    far_mixture = lax.ppermute(mix(far_blend, far_out).astype(jnp.bfloat16), "expert", across)
    mixture = mix(near_blend, near_out) + far_mixture.astype(jnp.float32)
    combined = hidden_state + mixture
    reward = jnp.sum(combined * reward_head.astype(jnp.float32), axis=-1)
    totals = jnp.sum(jnp.where(response_onehot, reward[:, None], 0.0), axis=0)
    counts = jnp.sum(response_onehot.astype(jnp.float32), axis=0)
    return (combined.astype(jnp.bfloat16), totals / counts)


def solution(mesh):
    in_specs = (
        P(("group", "expert"), None),
        P(("group", "expert"), None, None),
        P(),
        P(("group", "expert")),
        P(("group", "expert"), None),
        P(),
        P(),
        P(("group", "expert"), None),
        P("expert", None, None),
        P("expert", None, None),
        P("expert", None, None),
        P(),
    )
    out_specs = (P(("group", "expert"), None), P(("group", "expert")))
    return jax.shard_map(body, mesh=mesh, in_specs=in_specs, out_specs=out_specs, check_vma=False)
```

```python
import math

import jax
import jax.numpy as jnp
from jax import lax
from jax.sharding import PartitionSpec as P

epsilon = 1e-06


def expert_half(inputs, gate_rows, up_rows, down_rows):
    contract = (((1,), (1,)), ((), ()))
    gate_value = lax.dot_general(inputs, gate_rows, contract, preferred_element_type=jnp.float32)
    up_value = lax.dot_general(inputs, up_rows, contract, preferred_element_type=jnp.float32)
    active = (jax.nn.silu(gate_value) * up_value).astype(jnp.bfloat16)
    active = lax.optimization_barrier(active)
    return jnp.dot(active, down_rows, preferred_element_type=jnp.float32).astype(jnp.bfloat16)


def exchange(blocks, groups=None):
    return lax.all_to_all(
        blocks, "expert", split_axis=0, concat_axis=0, axis_index_groups=groups, tiled=True
    )


def slot_onehot(routes, first_expert, side_experts, capacity):
    token_count = routes.shape[0]
    expert_ids = first_expert + jnp.arange(side_experts, dtype=jnp.int32)
    member = jnp.any(routes[:, :, None] == expert_ids[None, None, :], axis=1)
    positions = jnp.arange(token_count, dtype=jnp.int32)
    before = (positions[None, :] < positions[:, None]).astype(jnp.bfloat16)
    place = jnp.dot(before, member.astype(jnp.bfloat16), preferred_element_type=jnp.float32)
    slot_ids = jnp.arange(capacity, dtype=jnp.int32).astype(jnp.float32)
    return member[:, :, None] & (place[:, :, None] == slot_ids[None, None, :])


def slot_blend(taken, normed, routes, router_weight, first_expert):
    token_count, side_experts, capacity = taken.shape
    logits = jnp.dot(normed, router_weight, preferred_element_type=jnp.float32)
    expert_ids = jnp.arange(router_weight.shape[1], dtype=jnp.int32)
    member = jnp.any(routes[:, :, None] == expert_ids[None, None, :], axis=1)
    chosen = jnp.where(member, jax.nn.sigmoid(logits), 0.0)
    route_weight = chosen / jnp.sum(chosen, axis=1, keepdims=True)
    route_weight = lax.dynamic_slice_in_dim(route_weight, first_expert, side_experts, axis=1)
    high = route_weight.astype(jnp.bfloat16)
    low = (route_weight - high.astype(jnp.float32)).astype(jnp.bfloat16)
    zero = jnp.zeros((), jnp.bfloat16)
    flat = (token_count, side_experts * capacity)
    return tuple(jnp.where(taken, part[:, :, None], zero).reshape(flat) for part in (high, low))


def with_context(rows, shard_rows, norm_gain):
    feature_count = norm_gain.shape[0]
    image_ids = jnp.arange(shard_rows.shape[0], dtype=jnp.int32).astype(jnp.float32)
    named = rows[:, feature_count : feature_count + 1].astype(jnp.float32)
    choose = (named == image_ids[None, :]).astype(jnp.bfloat16)
    context = jnp.dot(choose, shard_rows, preferred_element_type=jnp.float32)
    hidden = rows[:, :feature_count].astype(jnp.float32) + context
    inverse = lax.rsqrt(jnp.mean(hidden * hidden, axis=-1, keepdims=True) + epsilon)
    return hidden, (hidden * inverse * norm_gain.astype(jnp.float32)).astype(jnp.bfloat16)


def fill_slots(taken, normed):
    spread = taken.astype(jnp.bfloat16).reshape(taken.shape[0], -1)
    return lax.dot_general(
        spread, normed, (((0,), (0,)), ((), ())), preferred_element_type=jnp.float32
    ).astype(jnp.bfloat16)


def both_cores(mine, swap):
    return jnp.concatenate([mine, lax.ppermute(mine, "expert", swap)], axis=0)


def sum_cores(parts, swap):
    rows = parts.shape[0] // 2
    arrived = lax.ppermute(parts[rows:], "expert", swap)
    return (parts[:rows].astype(jnp.float32) + arrived.astype(jnp.float32)).astype(jnp.bfloat16)


def mix(blend, outputs):
    high, low = blend
    return jnp.dot(high, outputs, preferred_element_type=jnp.float32) + jnp.dot(
        low, outputs, preferred_element_type=jnp.float32
    )


def body(
    text_rows,
    image_rows,
    image_probe,
    response_image,
    token_response,
    norm_gain,
    router_weight,
    expert_routes,
    gate_weight,
    up_weight,
    down_weight,
    reward_head,
):
    token_count, feature_count = text_rows.shape
    top_count = expert_routes.shape[1]
    expert_count = router_weight.shape[1]
    capacity = min(token_count, 4 * token_count * top_count // (3 * expert_count))
    device_count = lax.axis_size("expert")
    response_count = response_image.shape[0]
    probe_score = jnp.einsum(
        "ivd,d->iv", image_rows, image_probe, preferred_element_type=jnp.float32
    )
    pool_weight = jax.nn.sigmoid(probe_score).astype(jnp.bfloat16)
    pooled_sum = jnp.einsum(
        "iv,ivd->id", pool_weight, image_rows, preferred_element_type=jnp.float32
    )
    pooled = (pooled_sum / math.sqrt(image_rows.shape[1])).astype(jnp.bfloat16)
    copies = jnp.broadcast_to(pooled[None], (device_count,) + pooled.shape)
    shard_rows = exchange(copies).reshape(-1, feature_count)
    response_onehot = (
        token_response[0][:, None] == jnp.arange(response_count, dtype=jnp.int32)[None, :]
    )
    token_image = jnp.sum(jnp.where(response_onehot, response_image[None, :], 0), axis=1)
    tag = jnp.broadcast_to(token_image[:, None], (token_count, 128)).astype(jnp.bfloat16)
    rows = jnp.concatenate([text_rows, tag], axis=1)
    side_experts = expert_count // 2
    half = device_count // 2
    first_expert = (lax.axis_index("expert") // half) * side_experts
    across = [(device, (device + half) % device_count) for device in range(device_count)]
    sides = [list(range(half)), list(range(half, device_count))]
    swap = [(device, device ^ 1) for device in range(device_count)]
    weights = (gate_weight[0], up_weight[0], down_weight[0])
    far_routes = lax.ppermute(expert_routes, "expert", across)
    far_rows = lax.ppermute(rows, "expert", across)
    near_taken = slot_onehot(expert_routes, first_expert, side_experts, capacity)
    far_taken = slot_onehot(far_routes, first_expert, side_experts, capacity)
    slot_total = side_experts * capacity
    flat = (slot_total, feature_count)
    blocks = (half, slot_total // half, feature_count)
    tagged_flat = (slot_total, rows.shape[1])
    tagged = (half, slot_total // half, rows.shape[1])
    near_slots = fill_slots(near_taken, rows).reshape(tagged)
    far_slots = fill_slots(far_taken, far_rows).reshape(tagged)
    near_slots, far_slots, shard_rows = lax.optimization_barrier(
        (near_slots, far_slots, shard_rows)
    )
    near_in = exchange(near_slots, sides).reshape(tagged_flat)
    near_in, far_slots = lax.optimization_barrier((both_cores(near_in, swap), far_slots))
    far_in = exchange(far_slots, sides).reshape(tagged_flat)
    near_input = with_context(near_in, shard_rows, norm_gain)[1]
    near_parts = expert_half(near_input, *weights)
    near_parts, far_in = lax.optimization_barrier((near_parts, far_in))
    near_sum = sum_cores(near_parts, swap)
    far_input = with_context(both_cores(far_in, swap), shard_rows, norm_gain)[1]
    far_sum = sum_cores(expert_half(far_input, *weights), swap)
    near_sum, far_sum = lax.optimization_barrier((near_sum, far_sum))
    far_out = exchange(far_sum.reshape(blocks), sides).reshape(flat)
    near_out = exchange(near_sum.reshape(blocks), sides).reshape(flat)
    hidden_state, normed = with_context(rows, shard_rows, norm_gain)
    far_normed = with_context(far_rows, shard_rows, norm_gain)[1]
    far_blend = slot_blend(far_taken, far_normed, far_routes, router_weight, first_expert)
    near_blend = slot_blend(near_taken, normed, expert_routes, router_weight, first_expert)
    far_mixture = lax.ppermute(mix(far_blend, far_out).astype(jnp.bfloat16), "expert", across)
    mixture = mix(near_blend, near_out) + far_mixture.astype(jnp.float32)
    combined = hidden_state + mixture
    reward = jnp.sum(combined * reward_head.astype(jnp.float32), axis=-1)
    totals = jnp.sum(jnp.where(response_onehot, reward[:, None], 0.0), axis=0)
    counts = jnp.sum(response_onehot.astype(jnp.float32), axis=0)
    return (combined.astype(jnp.bfloat16), totals / counts)


def solution(mesh):
    in_specs = (
        P(("group", "expert"), None),
        P(("group", "expert"), None, None),
        P(),
        P(("group", "expert")),
        P(("group", "expert"), None),
        P(),
        P(),
        P(("group", "expert"), None),
        P("expert", None, None),
        P("expert", None, None),
        P("expert", None, None),
        P(),
    )
    out_specs = (P(("group", "expert"), None), P(("group", "expert")))
    return jax.shard_map(body, mesh=mesh, in_specs=in_specs, out_specs=out_specs, check_vma=False)
```

```python
import math

import jax
import jax.numpy as jnp
from jax import lax
from jax.sharding import PartitionSpec as P

epsilon = 1e-06


def expert_half(inputs, gate_rows, up_rows, down_rows):
    contract = (((1,), (1,)), ((), ()))
    gate_value = lax.dot_general(inputs, gate_rows, contract, preferred_element_type=jnp.float32)
    up_value = lax.dot_general(inputs, up_rows, contract, preferred_element_type=jnp.float32)
    active = (jax.nn.silu(gate_value) * up_value).astype(jnp.bfloat16)
    active = lax.optimization_barrier(active)
    return jnp.dot(active, down_rows, preferred_element_type=jnp.float32).astype(jnp.bfloat16)


def exchange(blocks, groups=None):
    return lax.all_to_all(
        blocks, "expert", split_axis=0, concat_axis=0, axis_index_groups=groups, tiled=True
    )


def slot_onehot(routes, first_expert, side_experts, capacity):
    token_count = routes.shape[0]
    expert_ids = first_expert + jnp.arange(side_experts, dtype=jnp.int32)
    member = jnp.any(routes[:, :, None] == expert_ids[None, None, :], axis=1)
    positions = jnp.arange(token_count, dtype=jnp.int32)
    before = (positions[None, :] < positions[:, None]).astype(jnp.bfloat16)
    place = jnp.dot(before, member.astype(jnp.bfloat16), preferred_element_type=jnp.float32)
    slot_ids = jnp.arange(capacity, dtype=jnp.int32).astype(jnp.float32)
    return member[:, :, None] & (place[:, :, None] == slot_ids[None, None, :])


def slot_blend(taken, normed, routes, router_weight, first_expert):
    token_count, side_experts, capacity = taken.shape
    logits = jnp.dot(normed, router_weight, preferred_element_type=jnp.float32)
    expert_ids = jnp.arange(router_weight.shape[1], dtype=jnp.int32)
    member = jnp.any(routes[:, :, None] == expert_ids[None, None, :], axis=1)
    chosen = jnp.where(member, jax.nn.sigmoid(logits), 0.0)
    route_weight = chosen / jnp.sum(chosen, axis=1, keepdims=True)
    route_weight = lax.dynamic_slice_in_dim(route_weight, first_expert, side_experts, axis=1)
    high = route_weight.astype(jnp.bfloat16)
    low = (route_weight - high.astype(jnp.float32)).astype(jnp.bfloat16)
    zero = jnp.zeros((), jnp.bfloat16)
    flat = (token_count, side_experts * capacity)
    return tuple(jnp.where(taken, part[:, :, None], zero).reshape(flat) for part in (high, low))


def with_context(rows, shard_rows, norm_gain):
    feature_count = norm_gain.shape[0]
    image_ids = jnp.arange(shard_rows.shape[0], dtype=jnp.int32).astype(jnp.float32)
    named = rows[:, feature_count : feature_count + 1].astype(jnp.float32)
    choose = (named == image_ids[None, :]).astype(jnp.bfloat16)
    context = jnp.dot(choose, shard_rows, preferred_element_type=jnp.float32)
    hidden = rows[:, :feature_count].astype(jnp.float32) + context
    inverse = lax.rsqrt(jnp.mean(hidden * hidden, axis=-1, keepdims=True) + epsilon)
    return hidden, (hidden * inverse * norm_gain.astype(jnp.float32)).astype(jnp.bfloat16)


def fill_slots(taken, normed):
    spread = taken.astype(jnp.bfloat16).reshape(taken.shape[0], -1)
    return lax.dot_general(
        spread, normed, (((0,), (0,)), ((), ())), preferred_element_type=jnp.float32
    ).astype(jnp.bfloat16)


def both_cores(mine, swap):
    return jnp.concatenate([mine, lax.ppermute(mine, "expert", swap)], axis=0)


def sum_cores(parts, swap):
    rows = parts.shape[0] // 2
    arrived = lax.ppermute(parts[rows:], "expert", swap)
    return (parts[:rows].astype(jnp.float32) + arrived.astype(jnp.float32)).astype(jnp.bfloat16)


def mix(blend, outputs):
    high, low = blend
    return jnp.dot(high, outputs, preferred_element_type=jnp.float32) + jnp.dot(
        low, outputs, preferred_element_type=jnp.float32
    )


def body(
    text_rows,
    image_rows,
    image_probe,
    response_image,
    token_response,
    norm_gain,
    router_weight,
    expert_routes,
    gate_weight,
    up_weight,
    down_weight,
    reward_head,
):
    token_count, feature_count = text_rows.shape
    top_count = expert_routes.shape[1]
    expert_count = router_weight.shape[1]
    capacity = min(token_count, 4 * token_count * top_count // (3 * expert_count))
    device_count = lax.axis_size("expert")
    response_count = response_image.shape[0]
    probe_score = jnp.einsum(
        "ivd,d->iv", image_rows, image_probe, preferred_element_type=jnp.float32
    )
    pool_weight = jax.nn.sigmoid(probe_score).astype(jnp.bfloat16)
    pooled_sum = jnp.einsum(
        "iv,ivd->id", pool_weight, image_rows, preferred_element_type=jnp.float32
    )
    pooled = (pooled_sum / math.sqrt(image_rows.shape[1])).astype(jnp.bfloat16)
    copies = jnp.broadcast_to(pooled[None], (device_count,) + pooled.shape)
    shard_rows = exchange(copies).reshape(-1, feature_count)
    response_onehot = (
        token_response[0][:, None] == jnp.arange(response_count, dtype=jnp.int32)[None, :]
    )
    token_image = jnp.sum(jnp.where(response_onehot, response_image[None, :], 0), axis=1)
    tag = jnp.broadcast_to(token_image[:, None], (token_count, 128)).astype(jnp.bfloat16)
    rows = jnp.concatenate([text_rows, tag], axis=1)
    side_experts = expert_count // 2
    half = device_count // 2
    first_expert = (lax.axis_index("expert") // half) * side_experts
    across = [(device, (device + half) % device_count) for device in range(device_count)]
    sides = [list(range(half)), list(range(half, device_count))]
    swap = [(device, device ^ 1) for device in range(device_count)]
    weights = (gate_weight[0], up_weight[0], down_weight[0])
    far_routes = lax.ppermute(expert_routes, "expert", across)
    far_rows = lax.ppermute(rows, "expert", across)
    near_taken = slot_onehot(expert_routes, first_expert, side_experts, capacity)
    far_taken = slot_onehot(far_routes, first_expert, side_experts, capacity)
    slot_total = side_experts * capacity
    flat = (slot_total, feature_count)
    blocks = (half, slot_total // half, feature_count)
    tagged_flat = (slot_total, rows.shape[1])
    tagged = (half, slot_total // half, rows.shape[1])
    near_slots = fill_slots(near_taken, rows).reshape(tagged)
    far_slots = fill_slots(far_taken, far_rows).reshape(tagged)
    near_slots, shard_rows = lax.optimization_barrier((near_slots, shard_rows))
    near_in = exchange(near_slots, sides).reshape(tagged_flat)
    near_in, far_slots = lax.optimization_barrier((near_in, far_slots))
    near_in, far_slots = lax.optimization_barrier((both_cores(near_in, swap), far_slots))
    far_in = exchange(far_slots, sides).reshape(tagged_flat)
    near_input = with_context(near_in, shard_rows, norm_gain)[1]
    near_parts = expert_half(near_input, *weights)
    near_parts, far_in = lax.optimization_barrier((near_parts, far_in))
    near_sum = sum_cores(near_parts, swap)
    far_input = with_context(both_cores(far_in, swap), shard_rows, norm_gain)[1]
    far_sum = sum_cores(expert_half(far_input, *weights), swap)
    near_sum, far_sum = lax.optimization_barrier((near_sum, far_sum))
    far_out = exchange(far_sum.reshape(blocks), sides).reshape(flat)
    near_out = exchange(near_sum.reshape(blocks), sides).reshape(flat)
    hidden_state, normed = with_context(rows, shard_rows, norm_gain)
    far_normed = with_context(far_rows, shard_rows, norm_gain)[1]
    far_blend = slot_blend(far_taken, far_normed, far_routes, router_weight, first_expert)
    near_blend = slot_blend(near_taken, normed, expert_routes, router_weight, first_expert)
    far_mixture = lax.ppermute(mix(far_blend, far_out).astype(jnp.bfloat16), "expert", across)
    mixture = mix(near_blend, near_out) + far_mixture.astype(jnp.float32)
    combined = hidden_state + mixture
    reward = jnp.sum(combined * reward_head.astype(jnp.float32), axis=-1)
    totals = jnp.sum(jnp.where(response_onehot, reward[:, None], 0.0), axis=0)
    counts = jnp.sum(response_onehot.astype(jnp.float32), axis=0)
    return (combined.astype(jnp.bfloat16), totals / counts)


def solution(mesh):
    in_specs = (
        P(("group", "expert"), None),
        P(("group", "expert"), None, None),
        P(),
        P(("group", "expert")),
        P(("group", "expert"), None),
        P(),
        P(),
        P(("group", "expert"), None),
        P("expert", None, None),
        P("expert", None, None),
        P("expert", None, None),
        P(),
    )
    out_specs = (P(("group", "expert"), None), P(("group", "expert")))
    return jax.shard_map(body, mesh=mesh, in_specs=in_specs, out_specs=out_specs, check_vma=False)
```
